32 devices in a mesh: group: 2 (over x), row: 16 (over z, y, core).
Axes of the slice: x: 2, y: 2, z: 4, core: 2. Of those that a mesh axis runs over, the one named last changes fastest.
Arguments:
- factor_panel: bfloat16 [65536, 4096], P(('group', 'row')), parts along dimension 0, may hold values from -0.046875 to 0.046875
- right_side: float32 [65536, 256], P(('group', 'row')), parts along dimension 0, may hold values from -6 to 6
- solved_below: bfloat16 [65536, 256], P(('group', 'row')), parts along dimension 0, may hold values from -6 to 6
- diag_inverse: bfloat16 [32768, 1024], P(('group', 'row')), parts along dimension 0, may hold values from -1.5 to 1.5
Outputs:
- forward: float32 [65536, 256], P(('group', 'row')), parts along dimension 0
- solution: float32 [65536, 256], P(('group', 'row')), parts along dimension 0
The draws below stay inside these ranges and needn't reach their ends.
There are 2 independent parts, one for each index of `group`. The reference program is written for one: setup_inputs(seed, part) draws one part's arguments, and reference() takes and returns one part's arrays. A program takes and returns all parts, laid end to end along the dimension named above; each array names one. Nothing has to cross between parts.
All inputs are finite; a program needn't handle non-finite values.
Results may differ from the reference program's by a relative error of at most 0.0021.
Values may be sent and summed in bfloat16 or wider, within the bound.
A program may use at most 128 MiB of HBM per device.

```python
import jax
import jax.numpy as jnp

B = 1024
WB = 4
BPD = 2
R = 256
W = 4096
DIAG_ROWS = 16384
M = 32768


def draw_diag_inverse(key, part):
    key = jax.random.fold_in(key, 7)
    noise_key, diag_key = jax.random.split(key)
    noise = jnp.clip(jax.random.normal(noise_key, (DIAG_ROWS, B), jnp.float32), -4.0, 4.0)
    noise = noise * (0.25 / B ** 0.5)
    rows = jnp.arange(DIAG_ROWS)[:, None] % B
    cols = jnp.arange(B)[None, :]
    diag = jax.random.uniform(diag_key, (DIAG_ROWS, 1), jnp.float32, 0.6, 1.2)
    return (noise + jnp.where(rows == cols, diag, 0.0)).astype(jnp.bfloat16)


def block_scale(own_key, dims, cuts, least, top_value):
    level = 1.0
    for dim, shards_of in cuts:
        heights = jax.random.uniform(jax.random.fold_in(jax.random.fold_in(own_key, 6), dim), (shards_of,), jnp.float32, least / len(cuts), top_value / len(cuts))
        level = level * jnp.repeat(jnp.exp(heights), dims[dim] // shards_of).reshape((-1,) + (1,) * (len(dims) - 1 - dim))
    return level


def bell_draw(key, dims, width, most, cuts=(), kind=jnp.bfloat16):
    drawn = jax.random.normal(key, dims, jnp.float32) * width
    if len(cuts) > 0:
        drawn = block_scale(key, dims, cuts, -0.22, 0.18) * drawn
    return jnp.clip(drawn, min=-most, max=most).astype(kind)


def setup_inputs(seed: int = 0, part: int = 0) -> dict:
    key_list = jax.random.split(jax.random.key(seed), 5)
    own_keys = jax.random.split(jax.random.fold_in(key_list[4], part), 5)
    return {
        "factor_panel": bell_draw(own_keys[0], (M, W), (4 * W) ** -0.5, 0.046875, ((0, 16),)),
        "right_side": bell_draw(own_keys[1], (M, R), 1.0, 6.0, ((0, 16),), jnp.float32),
        "solved_below": bell_draw(own_keys[2], (M, R), 1.0, 6.0, ((0, 16),)),
        "diag_inverse": draw_diag_inverse(jax.random.fold_in(jax.random.fold_in(key_list[4], part), 71), part),
    }


def reference(factor_panel, right_side, solved_below, diag_inverse):
    rows_dev = BPD * B
    current = right_side
    forward_blocks = []
    for step in range(WB):
        lower = step * rows_dev
        solved = jnp.dot(diag_inverse[step * B:(step + 1) * B], current[lower:lower + B].astype(jnp.bfloat16), preferred_element_type=jnp.float32)
        forward_blocks.append(solved)
        current = current - jnp.dot(factor_panel[:, step * B:(step + 1) * B], solved.astype(jnp.bfloat16), preferred_element_type=jnp.float32)
    forward = current
    for step in range(WB):
        lower = step * rows_dev
        forward = forward.at[lower:lower + B].set(forward_blocks[step])
    row_ids = jnp.arange(factor_panel.shape[0], dtype=jnp.int32)
    in_window = jnp.logical_and(row_ids % rows_dev < B, row_ids // rows_dev < WB)
    known = jnp.where(in_window[:, None], jnp.zeros_like(solved_below), solved_below)
    trailing = jnp.dot(factor_panel.T, known, preferred_element_type=jnp.float32)
    rounded = [None] * WB
    exact = [None] * WB
    for step in reversed(range(WB)):
        total = trailing[step * B:(step + 1) * B]
        for later in range(step + 1, WB):
            lower = later * rows_dev
            total = total + jnp.dot(factor_panel[lower:lower + B, step * B:(step + 1) * B].T, rounded[later], preferred_element_type=jnp.float32)
        value = jnp.dot(diag_inverse[step * B:(step + 1) * B].T, (forward_blocks[step] - total).astype(jnp.bfloat16), preferred_element_type=jnp.float32)
        exact[step] = value
        rounded[step] = value.astype(jnp.bfloat16)
    solution = solved_below.astype(jnp.float32)
    for step in range(WB):
        lower = step * rows_dev
        solution = solution.at[lower:lower + B].set(exact[step])
    return forward, solution
```

```python
import functools

import jax
import jax.numpy as jnp
from jax import lax
from jax.experimental import pallas as pl
from jax.experimental.pallas import tpu as pltpu
from jax.sharding import PartitionSpec as P

F32 = jnp.float32
BF16 = jnp.bfloat16
NC = 4


def dot(a, b):
    return jnp.dot(a, b, preferred_element_type=F32)


def kernel(
    n, wb, l_hbm, rs_hbm, sb_hbm, d_hbm, fwd_hbm, sol_hbm,
    lv, cur, sb, sbt, dv, sol, keep, cstage, crecv, ysend, yrecv, zsend, zrecv,
    yb, cbf, vt, xt, ca, caf, cb, cbs,
    ld_sem, lf_sem, cs_sem, cr_sem, ys_sem, yr_sem, zs_sem, zr_sem, bs_sem, br_sem,
    cas_sem, car_sem, cbs_sem, cbr_sem,
):
    me = lax.axis_index("row")
    nq = n // wb
    q = me // wb
    j = me % wb
    j1 = j + 1 - 2 * (j % 2)
    j2 = (j + 2) % wb
    j3 = (j1 + 2) % wb
    base = me - j
    block = dv.shape[0]
    ck = block // NC
    rows = cur.shape[0]
    tiles = rows // ck

    def span(start, size=None):
        return pl.ds(pl.multiple_of(start, ck), ck if size is None else size)

    def loop(lo, hi, f):
        def step(i, _):
            f(i)
            return 0
        lax.fori_loop(lo, hi, step, 0)

    def remote(src, dst, ssem, rsem, to):
        return pltpu.make_async_remote_copy(
            src_ref=src, dst_ref=dst, send_sem=ssem, recv_sem=rsem,
            device_id={"row": to}, device_id_type=pl.DeviceIdType.MESH,
        )

    ld_d = pltpu.make_async_copy(d_hbm, dv, ld_sem.at[0])
    ld_r = pltpu.make_async_copy(rs_hbm, cur, ld_sem.at[1])
    ld_s = pltpu.make_async_copy(sb_hbm, sb, ld_sem.at[2])
    out_f = pltpu.make_async_copy(cur, fwd_hbm, ld_sem.at[3])
    out_s = pltpu.make_async_copy(sol, sol_hbm, ld_sem.at[4])

    def ld_l(h, b, c):
        where = (pl.ds(h * block, rows - block if h else block), span(b * block + c * ck))
        return pltpu.make_async_copy(l_hbm.at[where], lv.at[where], lf_sem.at[h, b, c])

    ld_r.start()
    ld_d.start()
    ld_s.start()
    loop(0, NC, lambda c: ld_l(0, 0, c).start())

    def load_rest(c):
        for b in range(wb):
            if b:
                ld_l(0, b, c).start()
            ld_l(1, b, c).start()
    loop(0, NC, load_rest)

    barrier = pltpu.get_barrier_semaphore()

    def greet(to):
        pl.semaphore_signal(barrier, inc=1, device_id={"row": to}, device_id_type=pl.DeviceIdType.MESH)

    greet(base + j1)
    greet(base + j2)
    greet(base + j3)

    @pl.when(q > 0)
    def _():
        greet(me - wb)

    @pl.when(q < nq - 1)
    def _():
        greet(me + wb)

    pl.semaphore_wait(barrier, 3 + jnp.where(q > 0, 1, 0) + jnp.where(q < nq - 1, 1, 0))

    def y_copy(way, k, c, to):
        part = yb.at[k, span(c * ck)]
        return remote(part, part, bs_sem.at[way, k, c], br_sem.at[k, c], to)

    def y_each(k, c, act):
        @pl.when(j % 2 == k % 2)
        def _():
            @pl.when((q == 0) & (j == k))
            def _():
                act(y_copy(1, k, c, base + j2))
            act(y_copy(0, k, c, base + j1))

            @pl.when(q < nq - 1)
            def _():
                act(y_copy(2, k, c, me + wb))

    def y_send(k, c):
        y_each(k, c, lambda copy: copy.start())

    def y_get(k, c):
        y_copy(0, k, c, base + j1).wait_recv()
        y_send(k, c)

    def get(k):
        loop(0, NC, lambda c: y_get(k, c))

    def absorb(k):
        def one(c):
            y_get(k, c)
            part = yb[k, span(c * ck)]

            def tile(t):
                r = span(t * ck)
                cur[r] = cur[r] - dot(lv[r, span(k * block + c * ck)], part)
            loop(0, NC, tile)
        loop(0, NC, one)

    def produce(k):
        cbf[...] = cur[0:block].astype(BF16)

        def one(c):
            r = span(c * ck)
            y = dot(dv[r], cbf[...])
            cur[r] = y
            yb[k, r] = y.astype(BF16)
            y_send(k, c)
        loop(0, NC, one)

    ld_r.wait()
    ld_d.wait()

    @pl.when(me == 0)
    def _():
        produce(0)

    loop(0, NC, lambda c: ld_l(0, 0, c).wait())

    @pl.when(me == 1)
    def _():
        absorb(0)
        produce(1)

    ld_s.wait()

    def turn(t):
        r = span(t * ck)
        x = sb[r].astype(F32)
        sol[r] = x
        first = (q == 0) & (t < NC)
        sbt[:, r] = jnp.where(first, jnp.zeros_like(x), x).T.astype(BF16)
    loop(0, tiles, turn)

    @pl.when(q > 0)
    def _():
        out_s.start()

    def c_copy(s, c):
        return remote(cstage.at[s, c], crecv.at[s, c], cs_sem.at[s, c], cr_sem.at[s, c], base + j1)

    def y_part(c):
        return remote(ysend.at[c], yrecv.at[c], ys_sem.at[c], yr_sem.at[c], base + j2)

    def z_copy(c, to):
        return remote(zsend.at[c], zrecv.at[c], zs_sem.at[c], zr_sem.at[c], to)

    def cross(c):
        c_copy(1, c).wait_recv()
        ysend[c] = (keep[1, c] + crecv[1, c].astype(F32)).astype(ysend.dtype)
        y_part(c).start()

    def partial(c):
        for b in range(wb):
            if b:
                ld_l(0, b, c).wait()
            ld_l(1, b, c).wait()

        def other(s):
            b = (j1 + 2 * s) % wb
            cstage[s, c] = dot(sbt[...], lv[:, span(b * block + c * ck)]).astype(cstage.dtype)
            c_copy(s, c).start()

        def own(s):
            b = (j + 2 * s) % wb
            keep[s, c] = dot(sbt[...], lv[:, span(b * block + c * ck)])
        loop(0, 2, lambda s: other(1 - s))
        loop(0, 2, lambda s: own(1 - s))
        cross(c)
    loop(0, NC, partial)

    @pl.when(me == 2)
    def _():
        absorb(0)
        absorb(1)
        produce(2)

    @pl.when(me == 3)
    def _():
        absorb(0)
        absorb(1)
        absorb(2)
        produce(3)

    def gemm(k):
        def tile(t):
            r = span(t * ck)
            cur[r] = cur[r] - dot(lv[r, k * block:(k + 1) * block], yb[k])
        loop(jnp.where(q == 0, NC, 0), tiles, tile)

    def tail(c):
        c_copy(0, c).wait_recv()
        total = keep[0, c] + crecv[0, c].astype(F32)
        y_part(c).wait_recv()
        keep[0, c] = total + yrecv[c].astype(F32)

        @pl.when(q < nq - 1)
        def _():
            z_copy(c, me + wb).wait_recv()
            keep[0, c] = keep[0, c] + zrecv[c].astype(F32)

        @pl.when(q > 0)
        def _():
            zsend[c] = keep[0, c].astype(zsend.dtype)
            z_copy(c, me - wb).start()

    def ca_copy(slot, c, to):
        return remote(caf.at[slot, c], ca.at[slot, c], cas_sem.at[slot, c], car_sem.at[slot, c], to)

    def cb_copy(slot, c, to):
        return remote(cbs.at[slot, c], cb.at[c], cbs_sem.at[slot, c], cbr_sem.at[c], to)

    def back(k):
        def rhs(c):
            s = keep[0, c]
            if k == 2:
                ca_copy(2, c, base + j1).wait_recv()
                s = s + ca[2, c]
            if k < 2:
                cb_copy(0, c, base + 2).wait_recv()
                s = s + cb[c].astype(F32)
            if k == 0:
                ca_copy(0, c, base + j1).wait_recv()
                s = s + ca[0, c]
            vt[:, span(c * ck)] = (cur[span(c * ck)].T - s).astype(BF16)
        loop(0, NC, rhs)

        def solve(c):
            x = dot(vt[...], dv[:, span(c * ck)])
            xt[:, span(c * ck)] = x.astype(BF16)
            sol[span(c * ck)] = x.T
        loop(0, NC, solve)
        for kk in reversed(range(k)):
            def give(c):
                value = dot(xt[...], lv[0:block, span(kk * block + c * ck)])
                if k == 2:
                    ca_copy(kk, c, base + j1).wait_recv()
                    cbs[kk, c] = (value + ca[kk, c]).astype(cbs.dtype)
                    cb_copy(kk, c, base + kk).start()
                else:
                    caf[kk, c] = value
                    ca_copy(kk, c, base + j1).start()
            loop(0, NC, give)
        out_s.start()

    @pl.when(q > 0)
    def _():
        loop(0, NC, tail)
        for k in range(wb):
            get(k)
            gemm(k)
        out_f.start()

    @pl.when(me == 0)
    def _():
        gemm(0)
        get(1)
        gemm(1)

    @pl.when(me == 1)
    def _():
        gemm(0)
        gemm(1)

    @pl.when(q == 0)
    def _():
        loop(0, NC, tail)

        @pl.when(j < 2)
        def _():
            for k in (2, 3):
                get(k)
                gemm(k)
            out_f.start()

        @pl.when(j == 0)
        def _():
            back(0)

        @pl.when(j == 1)
        def _():
            back(1)

        @pl.when(j == 2)
        def _():
            back(2)
            get(3)

        @pl.when(j == 3)
        def _():
            back(3)

        @pl.when(j >= 2)
        def _():
            for k in range(wb):
                gemm(k)
            out_f.start()

    def finish(c):
        c_copy(0, c).wait_send()
        c_copy(1, c).wait_send()
        y_part(c).wait_send()

        @pl.when(q > 0)
        def _():
            z_copy(c, me - wb).wait_send()
        for k in range(wb):
            y_each(k, c, lambda copy: copy.wait_send())

        @pl.when(me == 3)
        def _():
            for kk in range(3):
                ca_copy(kk, c, base + j1).wait_send()

        @pl.when(me == 2)
        def _():
            for kk in range(2):
                cb_copy(kk, c, base + kk).wait_send()

        @pl.when(me == 1)
        def _():
            ca_copy(0, c, base + j1).wait_send()
    loop(0, NC, finish)
    out_f.wait()
    out_s.wait()


def body(n, factor_panel, right_side, solved_below, diag_inverse):
    rows, width = factor_panel.shape
    block = diag_inverse.shape[1]
    wb = width // block
    cols = right_side.shape[1]
    ck = block // NC
    piece = (NC, cols, ck)
    dma = pltpu.SemaphoreType.DMA
    out = jax.ShapeDtypeStruct(right_side.shape, F32)
    return tuple(pl.pallas_call(
        functools.partial(kernel, n, wb),
        out_shape=(out, out),
        in_specs=[pl.BlockSpec(memory_space=pl.ANY)] * 4,
        out_specs=(pl.BlockSpec(memory_space=pl.ANY),) * 2,
        scratch_shapes=[
            pltpu.VMEM((rows, width), BF16),
            pltpu.VMEM((rows, cols), F32),
            pltpu.VMEM((rows, cols), BF16),
            pltpu.VMEM((cols, rows), BF16),
            pltpu.VMEM((block, block), BF16),
            pltpu.VMEM((rows, cols), F32),
            pltpu.VMEM((2,) + piece, F32),
            pltpu.VMEM((2,) + piece, F32),
            pltpu.VMEM((2,) + piece, F32),
            pltpu.VMEM(piece, BF16),
            pltpu.VMEM(piece, BF16),
            pltpu.VMEM(piece, F32),
            pltpu.VMEM(piece, F32),
            pltpu.VMEM((wb, block, cols), BF16),
            pltpu.VMEM((block, cols), BF16),
            pltpu.VMEM((cols, block), BF16),
            pltpu.VMEM((cols, block), BF16),
            pltpu.VMEM((3,) + piece, F32),
            pltpu.VMEM((3,) + piece, F32),
            pltpu.VMEM(piece, BF16),
            pltpu.VMEM((2,) + piece, BF16),
            dma((5,)), dma((2, wb, NC)),
            dma((2, NC)), dma((2, NC)),
            dma((NC,)), dma((NC,)), dma((NC,)), dma((NC,)),
            dma((3, wb, NC)), dma((wb, NC)),
            dma((3, NC)), dma((3, NC)), dma((2, NC)), dma((NC,)),
        ],
        compiler_params=pltpu.CompilerParams(
            collective_id=0, has_side_effects=True, vmem_limit_bytes=60 * 1024 * 1024
        ),
        cost_estimate=pl.CostEstimate(
            flops=4 * rows * width * cols, bytes_accessed=2 * rows * width, transcendentals=0
        ),
    )(factor_panel, right_side, solved_below, diag_inverse))


def solution(mesh):
    spec = P(("group", "row"), None)
    return jax.shard_map(
        functools.partial(body, mesh.shape["row"]),
        mesh=mesh, in_specs=(spec,) * 4, out_specs=(spec,) * 2, check_vma=False,
    )
```

```python
import functools

import jax
import jax.numpy as jnp
from jax import lax
from jax.experimental import pallas as pl
from jax.experimental.pallas import tpu as pltpu
from jax.sharding import PartitionSpec as P

F32 = jnp.float32
BF16 = jnp.bfloat16
NC = 4
NF = 2


def dot(a, b):
    return jnp.dot(a, b, preferred_element_type=F32)


def kernel(
    n, wb, l_hbm, rs_hbm, sb_hbm, d_hbm, fwd_hbm, sol_hbm,
    lv, cur, sb, sbt, dv, sol, keep, cstage, crecv, ysend, yrecv, zsend, zrecv,
    zsend_b, zrecv_b, yb, cbf, vt, xt, ca, caf, cb, cbs,
    ld_sem, lf_sem, cs_sem, cr_sem, ys_sem, yr_sem, zs_sem, zr_sem, bs_sem, br_sem,
    cas_sem, car_sem, cbs_sem, cbr_sem,
):
    me = lax.axis_index("row")
    nq = n // wb
    q = me // wb
    j = me % wb
    j1 = j + 1 - 2 * (j % 2)
    j2 = (j + 2) % wb
    j3 = (j1 + 2) % wb
    base = me - j
    block = dv.shape[0]
    ck = block // NC
    rows = cur.shape[0]
    tiles = rows // ck

    def span(start, size=None):
        return pl.ds(pl.multiple_of(start, ck), ck if size is None else size)

    def loop(lo, hi, f):
        def step(i, _):
            f(i)
            return 0
        lax.fori_loop(lo, hi, step, 0)

    def remote(src, dst, ssem, rsem, to):
        return pltpu.make_async_remote_copy(
            src_ref=src, dst_ref=dst, send_sem=ssem, recv_sem=rsem,
            device_id={"row": to}, device_id_type=pl.DeviceIdType.MESH,
        )

    ld_d = pltpu.make_async_copy(d_hbm, dv, ld_sem.at[0])
    ld_r = pltpu.make_async_copy(rs_hbm, cur, ld_sem.at[1])
    ld_s = pltpu.make_async_copy(sb_hbm, sb, ld_sem.at[2])
    out_f = pltpu.make_async_copy(cur, fwd_hbm, ld_sem.at[3])
    out_s = pltpu.make_async_copy(sol, sol_hbm, ld_sem.at[4])

    def ld_l(h, b, c):
        where = (pl.ds(h * block, rows - block if h else block), span(b * block + c * ck))
        return pltpu.make_async_copy(l_hbm.at[where], lv.at[where], lf_sem.at[h, b, c])

    ld_r.start()
    ld_d.start()
    ld_s.start()
    barrier = pltpu.get_barrier_semaphore()

    def greet(to):
        pl.semaphore_signal(barrier, inc=1, device_id={"row": to}, device_id_type=pl.DeviceIdType.MESH)

    greet(base + j1)
    greet(base + j2)
    greet(base + j3)

    @pl.when(q > 0)
    def _():
        greet(me - wb)

    @pl.when(q < nq - 1)
    def _():
        greet(me + wb)

    pl.semaphore_wait(barrier, 3 + jnp.where(q > 0, 1, 0) + jnp.where(q < nq - 1, 1, 0))

    loop(0, NC, lambda c: ld_l(0, 0, c).start())

    def load_rest(c):
        for b in range(wb):
            if b:
                ld_l(0, b, c).start()
            ld_l(1, b, c).start()
    loop(0, NC, load_rest)

    def y_copy(way, k, c, to):
        part = yb.at[k, span(c * ck)]
        return remote(part, part, bs_sem.at[way, k, c], br_sem.at[k, c], to)

    def y_each(k, c, act):
        @pl.when(j % 2 == k % 2)
        def _():
            @pl.when((q == 0) & (j == k))
            def _():
                act(y_copy(1, k, c, base + j2))
            act(y_copy(0, k, c, base + j1))

            @pl.when(q < nq - 1)
            def _():
                act(y_copy(2, k, c, me + wb))

    def y_send(k, c):
        y_each(k, c, lambda copy: copy.start())

    def y_get(k, c):
        y_copy(0, k, c, base + j1).wait_recv()
        y_send(k, c)

    def get(k):
        loop(0, NC, lambda c: y_get(k, c))

    def absorb(k):
        def one(c):
            y_get(k, c)
            part = yb[k, span(c * ck)]
            cur[0:block] = cur[0:block] - dot(lv[0:block, span(k * block + c * ck)], part)
        loop(0, NC, one)

    def produce(k):
        cbf[...] = cur[0:block].astype(BF16)

        def one(c):
            r = span(c * ck)
            y = dot(dv[r], cbf[...])
            cur[r] = y
            yb[k, r] = y.astype(BF16)
            y_send(k, c)
        loop(0, NC, one)

    ld_r.wait()
    ld_d.wait()

    @pl.when(me == 0)
    def _():
        produce(0)
        get(1)

    loop(0, NC, lambda c: ld_l(0, 0, c).wait())

    @pl.when(me == 1)
    def _():
        absorb(0)
        produce(1)

    ld_s.wait()

    def turn(t):
        r = span(t * ck)
        x = sb[r].astype(F32)
        sol[r] = x
        first = (q == 0) & (t < NC)
        sbt[:, r] = jnp.where(first, jnp.zeros_like(x), x).T.astype(BF16)
    loop(0, tiles, turn)

    @pl.when(q > 0)
    def _():
        out_s.start()

    def c_copy(s, c):
        return remote(cstage.at[s, c], crecv.at[s, c], cs_sem.at[s, c], cr_sem.at[s, c], base + j1)

    def y_part(c):
        return remote(ysend.at[c], yrecv.at[c], ys_sem.at[c], yr_sem.at[c], base + j2)

    def z_copy(c, to):
        return remote(zsend.at[c], zrecv.at[c], zs_sem.at[c], zr_sem.at[c], to)

    def z_copy_b(c, to):
        return remote(zsend_b.at[c], zrecv_b.at[c], zs_sem.at[c], zr_sem.at[c], to)

    def cross(c):
        c_copy(1, c).wait_recv()
        ysend[c] = (keep[1, c] + crecv[1, c].astype(F32)).astype(ysend.dtype)
        y_part(c).start()

    last = q == nq - 1

    def tail(c):
        c_copy(0, c).wait_recv()
        total = keep[0, c] + crecv[0, c].astype(F32)
        y_part(c).wait_recv()
        keep[0, c] = total + yrecv[c].astype(F32)

        @pl.when(q < nq - 1)
        def _():
            @pl.when(c < NF)
            def _():
                z_copy(c, me + wb).wait_recv()
                keep[0, c] = keep[0, c] + zrecv[c]

            @pl.when(c >= NF)
            def _():
                z_copy_b(c, me + wb).wait_recv()
                keep[0, c] = keep[0, c] + zrecv_b[c].astype(F32)

        @pl.when(q > 0)
        def _():
            @pl.when(c < NF)
            def _():
                zsend[c] = keep[0, c]
                z_copy(c, me - wb).start()

            @pl.when(c >= NF)
            def _():
                zsend_b[c] = keep[0, c].astype(BF16)
                z_copy_b(c, me - wb).start()

    def partial(c):
        for b in range(wb):
            if b:
                ld_l(0, b, c).wait()
            ld_l(1, b, c).wait()

        def other(s):
            b = (j1 + 2 * s) % wb
            cstage[s, c] = dot(sbt[...], lv[:, span(b * block + c * ck)]).astype(cstage.dtype)
            c_copy(s, c).start()

        def own(s):
            b = (j + 2 * s) % wb
            keep[s, c] = dot(sbt[...], lv[:, span(b * block + c * ck)])
        loop(0, 2, lambda s: other(1 - s))
        loop(0, 2, lambda s: own(1 - s))
        cross(c)

        @pl.when(last & (c > 0))
        def _():
            tail(c - 1)
    loop(0, NC, partial)

    @pl.when(me == 2)
    def _():
        absorb(0)
        absorb(1)
        produce(2)

    @pl.when(me == 3)
    def _():
        absorb(0)
        absorb(1)
        absorb(2)
        produce(3)

    def gemm(k):
        def tile(t):
            r = span(t * ck)
            cur[r] = cur[r] - dot(lv[r, k * block:(k + 1) * block], yb[k])
        loop(jnp.where(q == 0, NC, 0), tiles, tile)

    def ca_copy(slot, c, to):
        return remote(caf.at[slot, c], ca.at[slot, c], cas_sem.at[slot, c], car_sem.at[slot, c], to)

    def cb_copy(slot, c, to):
        return remote(cbs.at[slot, c], cb.at[c], cbs_sem.at[slot, c], cbr_sem.at[c], to)

    def back(k):
        def rhs(c):
            s = keep[0, c]
            if k == 2:
                ca_copy(2, c, base + j1).wait_recv()
                s = s + ca[2, c]
            if k < 2:
                cb_copy(0, c, base + 2).wait_recv()
                s = s + cb[c].astype(F32)
            if k == 0:
                ca_copy(0, c, base + j1).wait_recv()
                s = s + ca[0, c]
            vt[:, span(c * ck)] = (cur[span(c * ck)].T - s).astype(BF16)
        loop(0, NC, rhs)

        def solve(c):
            x = dot(vt[...], dv[:, span(c * ck)])
            xt[:, span(c * ck)] = x.astype(BF16)
            sol[span(c * ck)] = x.T
        loop(0, NC, solve)
        for kk in reversed(range(k)):
            def give(c):
                value = dot(xt[...], lv[0:block, span(kk * block + c * ck)])
                if k == 2:
                    ca_copy(kk, c, base + j1).wait_recv()
                    cbs[kk, c] = (value + ca[kk, c]).astype(cbs.dtype)
                    cb_copy(kk, c, base + kk).start()
                else:
                    caf[kk, c] = value
                    ca_copy(kk, c, base + j1).start()
            loop(0, NC, give)
        out_s.start()

    def carried(low, ours):
        for k in (low, low + 1):
            @pl.when((j % 2 == k % 2) if ours else (j % 2 != k % 2))
            def _():
                get(k)

    @pl.when(q > 0)
    def _():
        @pl.when((q == 1) & ~last)
        def _():
            carried(0, True)
        loop(jnp.where(last, NC - 1, 0), NC // 2, tail)

        @pl.when((q > 1) & ~last)
        def _():
            carried(0, True)
        loop(jnp.where(last, NC - 1, NC // 2), NC, tail)

        @pl.when(last)
        def _():
            carried(0, True)

        @pl.when(~last)
        def _():
            carried(2, True)
        carried(0, False)
        gemm(0)
        gemm(1)

        @pl.when(last)
        def _():
            carried(2, True)
        carried(2, False)
        gemm(2)
        gemm(3)
        out_f.start()

    @pl.when(me == 0)
    def _():
        gemm(0)
        gemm(1)

    @pl.when(me == 1)
    def _():
        gemm(0)
        gemm(1)

    @pl.when(q == 0)
    def _():
        loop(0, NC, tail)

        @pl.when(j < 2)
        def _():
            for k in (2, 3):
                get(k)
                gemm(k)
            out_f.start()

        @pl.when(j == 0)
        def _():
            back(0)

        @pl.when(j == 1)
        def _():
            back(1)

        @pl.when(j == 2)
        def _():
            back(2)
            get(3)

        @pl.when(j == 3)
        def _():
            back(3)

        @pl.when(j >= 2)
        def _():
            for k in range(wb):
                gemm(k)
            out_f.start()

    def finish(c):
        c_copy(0, c).wait_send()
        c_copy(1, c).wait_send()
        y_part(c).wait_send()

        @pl.when(q > 0)
        def _():
            @pl.when(c < NF)
            def _():
                z_copy(c, me - wb).wait_send()

            @pl.when(c >= NF)
            def _():
                z_copy_b(c, me - wb).wait_send()
        for k in range(wb):
            y_each(k, c, lambda copy: copy.wait_send())

        @pl.when(me == 3)
        def _():
            for kk in range(3):
                ca_copy(kk, c, base + j1).wait_send()

        @pl.when(me == 2)
        def _():
            for kk in range(2):
                cb_copy(kk, c, base + kk).wait_send()

        @pl.when(me == 1)
        def _():
            ca_copy(0, c, base + j1).wait_send()
    loop(0, NC, finish)
    out_f.wait()
    out_s.wait()


def body(n, factor_panel, right_side, solved_below, diag_inverse):
    rows, width = factor_panel.shape
    block = diag_inverse.shape[1]
    wb = width // block
    cols = right_side.shape[1]
    ck = block // NC
    piece = (NC, cols, ck)
    dma = pltpu.SemaphoreType.DMA
    out = jax.ShapeDtypeStruct(right_side.shape, F32)
    return tuple(pl.pallas_call(
        functools.partial(kernel, n, wb),
        out_shape=(out, out),
        in_specs=[pl.BlockSpec(memory_space=pl.ANY)] * 4,
        out_specs=(pl.BlockSpec(memory_space=pl.ANY),) * 2,
        scratch_shapes=[
            pltpu.VMEM((rows, width), BF16),
            pltpu.VMEM((rows, cols), F32),
            pltpu.VMEM((rows, cols), BF16),
            pltpu.VMEM((cols, rows), BF16),
            pltpu.VMEM((block, block), BF16),
            pltpu.VMEM((rows, cols), F32),
            pltpu.VMEM((2,) + piece, F32),
            pltpu.VMEM((2,) + piece, F32),
            pltpu.VMEM((2,) + piece, F32),
            pltpu.VMEM(piece, F32),
            pltpu.VMEM(piece, F32),
            pltpu.VMEM(piece, F32),
            pltpu.VMEM(piece, F32),
            pltpu.VMEM(piece, BF16),
            pltpu.VMEM(piece, BF16),
            pltpu.VMEM((wb, block, cols), BF16),
            pltpu.VMEM((block, cols), BF16),
            pltpu.VMEM((cols, block), BF16),
            pltpu.VMEM((cols, block), BF16),
            pltpu.VMEM((3,) + piece, F32),
            pltpu.VMEM((3,) + piece, F32),
            pltpu.VMEM(piece, BF16),
            pltpu.VMEM((2,) + piece, BF16),
            dma((5,)), dma((2, wb, NC)),
            dma((2, NC)), dma((2, NC)),
            dma((NC,)), dma((NC,)), dma((NC,)), dma((NC,)),
            dma((3, wb, NC)), dma((wb, NC)),
            dma((3, NC)), dma((3, NC)), dma((2, NC)), dma((NC,)),
        ],
        compiler_params=pltpu.CompilerParams(
            collective_id=0, has_side_effects=True, vmem_limit_bytes=50 * 1024 * 1024
        ),
        cost_estimate=pl.CostEstimate(
            flops=4 * rows * width * cols, bytes_accessed=2 * rows * width, transcendentals=0
        ),
    )(factor_panel, right_side, solved_below, diag_inverse))


def solution(mesh):
    spec = P(("group", "row"), None)
    return jax.shard_map(
        functools.partial(body, mesh.shape["row"]),
        mesh=mesh, in_specs=(spec,) * 4, out_specs=(spec,) * 2, check_vma=False,
    )
```
